32 devices in a mesh: groups: 1, expert: 16 (over z, y, x), tensor: 2 (over core).
Axes of the slice: x: 2, y: 2, z: 4, core: 2. Of those that a mesh axis runs over, the one named last changes fastest.
Arguments:
- tokens: bfloat16 [256, 2048], P(('groups', 'expert'), 'tensor'), may hold values from -6 to 6
- expert_ids: int32 [256, 8], P(('groups', 'expert')), may hold values from 0 to 15, all different within a row; in each aligned block of 16 rows (0 to 15, 16 to 31, ...) at most 11 rows name the same one
- route_weights: float32 [256, 8], P(('groups', 'expert')), may hold values from 0.05 to 0.5
- gate_weight: bfloat16 [16, 2048, 768], P('expert', None, 'tensor'), may hold values from -0.125 to 0.125
- up_weight: bfloat16 [16, 2048, 768], P('expert', None, 'tensor'), may hold values from -0.125 to 0.125
- down_weight: bfloat16 [16, 768, 2048], P('expert', 'tensor'), may hold values from -0.21875 to 0.21875
Outputs:
- mixed: bfloat16 [256, 2048], P(('groups', 'expert'), 'tensor')
The draws below stay inside these ranges and needn't reach their ends.
Inputs may be any that keep to these rules, and one draw needn't show every extreme that they name: `expert_ids`: each row names 8 different experts. In each aligned block of 16 rows no expert is named by more than 11 rows, and in some block an expert is named by exactly 11 rows.
All inputs are finite; a program needn't handle non-finite values.
Results may differ from the reference program's by a relative error of at most 0.005.
Values may be sent and summed in bfloat16 or wider, within the bound.
A program may use at most 64 MiB of HBM per device.

```python
import math
import jax
import jax.numpy as jnp
import numpy as np
from jax import lax

D = 2048
FF = 768
TOPK = 8
TOK_DEV = 16
EXPERTS = 16
BLOCKS = 16
TOKENS = 256
CAP = 11
SLOTS = 176


def levels(rng, dims, shards, low, top_value):
    def one(axis_at, shards_of):
        steps = jax.random.uniform(jax.random.fold_in(jax.random.fold_in(rng, 6), axis_at), (shards_of,), jnp.float32, low / len(shards), top_value / len(shards))
        return jnp.repeat(jnp.exp(steps), dims[axis_at] // shards_of).reshape((-1,) + (1,) * (len(dims) - axis_at - 1))

    gain = one(*shards[0])
    for cut in shards[1:]:
        gain = gain * one(*cut)
    return gain


def routed_block(key, own, number, rows, number_of, top, most, slope):
    sequence = jax.random.permutation(key, number_of)
    packed, usual = shares(number_of, rows * top, most, slope, True), shares(number_of, rows * top, most, slope, False)
    places = jnp.arange(number_of)

    def named(sizes, rotation):
        used = int((sizes > 0).sum())
        fixed = max(1, used // 4)
        shifted = fixed + (places - fixed + rotation * (used - fixed)) % max(1, number_of - fixed)
        return jnp.zeros((number_of,), jnp.int32).at[sequence[jnp.where(places < fixed, places, shifted)]].set(jnp.asarray(sizes, jnp.int32))

    sizes = jnp.where(number % 4 == 0, named(packed, number // 4), named(usual, number - number // 4 - 1))
    mixed = jax.random.permutation(jax.random.fold_in(own, 3), number_of)
    donor, sink = mixed[0:number_of // 2 * 2:2], mixed[1:number_of // 2 * 2:2]
    room = jnp.minimum(sizes[donor] - 1, most - sizes[sink]) // 2
    room = jnp.where((donor == sequence[0]) | (sink == sequence[0]) | (sizes[sink] == 0), 0, jnp.maximum(room, 0))
    shifted = jax.random.randint(jax.random.fold_in(own, 4), (number_of // 2,), 0, 1 << 20) % (room + 1)
    sizes = sizes.at[donor].add(-shifted).at[sink].add(shifted)
    labels = jnp.searchsorted(jnp.cumsum(sizes), jnp.arange(rows * top), side="right").astype(jnp.int32)
    table = labels.reshape(top, rows).T
    table = table[jax.random.permutation(jax.random.fold_in(own, 1), rows)]
    rotation = jax.random.randint(jax.random.fold_in(own, 2), (rows, 1), 0, top)
    return jnp.take_along_axis(table, (jnp.arange(top)[None, :] + rotation) % top, axis=1)


def shares(number_of, total, most, skew, full):
    loads = [(1 << 20) // math.isqrt(rank ** skew) + 1 for rank in range(1, number_of + 1)]
    largest = most if full else min(most, max(-(-total // number_of), total * loads[0] // sum(loads)))
    least = 1 if total - largest >= number_of - 1 else 0
    holding, surplus = [largest] + [least] * (number_of - 1), total - largest - least * (number_of - 1)
    while surplus > 0:
        movable = [i for i in range(1, number_of) if holding[i] < largest] or [i for i in range(1, number_of) if holding[i] < most]
        mass, budget = sum([loads[i] for i in movable]), surplus
        for i in movable:
            more = min(most - holding[i], max(1, budget * loads[i] // mass), surplus)
            holding[i] = holding[i] + more
            surplus = surplus - more
    return np.array(holding)


def normal_values(key, shape, scale, most, cuts=(), held_as=jnp.bfloat16):
    level = levels(key, shape, cuts, -0.22, 0.18) if cuts else 1.0
    values = jax.random.normal(key, shape, jnp.float32) * scale * level
    return jnp.minimum(jnp.maximum(values, -most), most).astype(held_as)


def setup_inputs(seed: int = 0, part: int = 0) -> dict:
    seeds = jax.random.split(jax.random.key(seed), 7)
    part_keys = jax.random.split(jax.random.fold_in(seeds[6], part), 7)
    tokens = normal_values(part_keys[0], (TOKENS, D), 1.0, 6.0, ((0, 16), (1, 2)))
    expert_ids_keys = jax.random.split(jax.random.fold_in(part_keys[1], 1), TOKENS // TOK_DEV)
    expert_ids_turns = jax.random.permutation(jax.random.fold_in(part_keys[1], 3), TOKENS // TOK_DEV)
    expert_ids = jax.vmap(lambda own, number: routed_block(jax.random.fold_in(part_keys[1], 2), own, number, TOK_DEV, EXPERTS, TOPK, CAP, 2))(expert_ids_keys, expert_ids_turns).reshape((TOKENS, TOPK))
    route_weights = jnp.clip(jnp.exp(math.log(0.5) - 2.3025851 * jax.random.uniform(part_keys[2], (TOKENS, TOPK), jnp.float32) ** levels(part_keys[2], (TOKENS, TOPK), ((0, 16),), -0.2, 0.2)), 0.05, 0.5)
    gate_weight = normal_values(seeds[3], (EXPERTS, D, FF), D ** -0.5, 0.125, ((0, 16), (2, 2)))
    up_weight = normal_values(seeds[4], (EXPERTS, D, FF), D ** -0.5, 0.125, ((0, 16), (2, 2)))
    down_weight = normal_values(seeds[5], (EXPERTS, FF, D), FF ** -0.5, 0.21875, ((0, 16), (1, 2)))
    return {"tokens": tokens, "expert_ids": expert_ids, "route_weights": route_weights, "gate_weight": gate_weight, "up_weight": up_weight, "down_weight": down_weight}


def slots_of(expert_ids):
    expert_range = jnp.arange(EXPERTS, dtype=jnp.int32)
    member_of = (expert_ids[:, :, None] == expert_range[None, None, :]).astype(jnp.int32)
    tallies = jnp.sum(member_of, axis=1).reshape(BLOCKS, TOK_DEV, EXPERTS)
    preceding = (jnp.cumsum(tallies, axis=1) - tallies).reshape(TOKENS, EXPERTS)
    return jnp.sum(member_of * preceding[:, None, :], axis=-1).astype(jnp.int32)


def reference(tokens, expert_ids, route_weights, gate_weight, up_weight, down_weight):
    slot_index = slots_of(expert_ids)
    token_range = jnp.arange(TOKENS, dtype=jnp.int32)
    block_of = (token_range // TOK_DEV).astype(jnp.int32)
    row_position = (block_of[:, None] * CAP + slot_index).astype(jnp.int32)
    token_position = jnp.broadcast_to(token_range[:, None], (TOKENS, TOPK)).astype(jnp.int32)
    source_table = jnp.full((EXPERTS, SLOTS), TOKENS, dtype=jnp.int32)
    source_table = source_table.at[expert_ids, row_position].set(token_position)
    weight_table = jnp.zeros((EXPERTS, SLOTS), dtype=jnp.float32)
    weight_table = weight_table.at[expert_ids, row_position].set(route_weights)
    padded = jnp.concatenate([tokens, jnp.zeros((1, D), dtype=tokens.dtype)], axis=0)

    def expert_step(total, pieces):
        gate_w, up_w, down_w, source_rows, weights_rows = pieces
        rows_in = padded[source_rows]
        gate_act = jnp.dot(rows_in, gate_w, preferred_element_type=jnp.float32)
        up_act = jnp.dot(rows_in, up_w, preferred_element_type=jnp.float32)
        hidden = (jax.nn.silu(gate_act) * up_act).astype(jnp.bfloat16)
        outputs = jnp.dot(hidden, down_w, preferred_element_type=jnp.float32)
        return total.at[source_rows].add(weights_rows[:, None] * outputs), None

    start_total = jnp.zeros((TOKENS + 1, D), dtype=jnp.float32)
    total, unused = lax.scan(expert_step, start_total, (gate_weight, up_weight, down_weight, source_table, weight_table))
    return total[:TOKENS].astype(jnp.bfloat16)
```

```python
import functools

import jax
import jax.numpy as jnp
from jax import lax
from jax.experimental import pallas as pl
from jax.experimental.pallas import tpu as pltpu
from jax.sharding import PartitionSpec as P

MESH = pl.DeviceIdType.MESH
BF16 = jnp.bfloat16
F32 = jnp.float32


def per_device(tokens, expert_ids, route_weights, gate_weight, up_weight, down_weight):
    tok_rows = tokens.shape[0]
    top_count = expert_ids.shape[1]
    expert_count = lax.axis_size("expert")
    capacity = min(
        tok_rows, max(2, (4 * tok_rows * top_count + 3 * expert_count - 1) // (3 * expert_count))
    )
    expert_range = jnp.arange(expert_count, dtype=jnp.int32)
    member_of = (expert_ids[:, :, None] == expert_range[None, None, :]).astype(jnp.int32)
    tallies = jnp.sum(member_of, axis=1)
    preceding = jnp.cumsum(tallies, axis=0) - tallies
    slot_index = jnp.sum(member_of * preceding[:, None, :], axis=-1)
    target_row = expert_ids * capacity + slot_index
    row_index = jnp.arange(expert_count * capacity, dtype=jnp.int32)
    placing = jnp.any(target_row[None, :, :] == row_index[:, None, None], axis=-1).astype(
        jnp.bfloat16
    )
    outgoing = jnp.dot(placing, tokens, preferred_element_type=jnp.float32).astype(jnp.bfloat16)
    outgoing = outgoing.reshape(expert_count, capacity, tokens.shape[1])
    incoming = lax.all_to_all(outgoing, "expert", split_axis=0, concat_axis=0, tiled=True)
    incoming = lax.all_gather(incoming, "tensor", axis=2, tiled=True)
    senders = incoming.shape[0]
    items = incoming.shape[1]
    stacked = incoming.reshape(senders * items, incoming.shape[2])
    gate_act = jnp.dot(stacked, gate_weight[0], preferred_element_type=jnp.float32)
    up_act = jnp.dot(stacked, up_weight[0], preferred_element_type=jnp.float32)
    hidden = (jax.nn.silu(gate_act) * up_act).astype(jnp.bfloat16)
    partial_value = jnp.dot(hidden, down_weight[0], preferred_element_type=jnp.float32)
    partial_value = partial_value.reshape(senders, items, partial_value.shape[1])
    returned = lax.all_to_all(partial_value, "expert", split_axis=0, concat_axis=0, tiled=True)
    returned = returned.reshape(expert_count * capacity, returned.shape[2])
    picked = jnp.take(returned, target_row.reshape(-1), axis=0).reshape(
        tok_rows, top_count, returned.shape[1]
    )
    mixed = jnp.sum(route_weights[:, :, None] * picked, axis=1)
    mixed = lax.psum_scatter(mixed, "tensor", scatter_dimension=1, tiled=True)
    return mixed.astype(jnp.bfloat16)


def kernel(
    tok_ref, ids_ref, rw_ref, gate_hbm, up_hbm, down_hbm, out_ref,
    xg, gu, dw, hid, ysend, p1, p2s, p2r,
    wsem, zs, zr, xs, xr, ys, yr, ds, dr, ps, pr, dws, dwr, hs, hr, as_, ar, bs, br,
):
    T = tok_ref.shape[0]
    DH = tok_ref.shape[1]
    F = gate_hbm.shape[2]
    me = lax.axis_index("expert")
    c = lax.axis_index("tensor")
    x = me % 2
    y = (me // 2) % 2
    z = me // 4
    zd = [z, z + 1 - 2 * (z % 2), (z + 2) % 4, 3 - z]
    plane = y * 2 + x
    xn = y * 2 + 1 - x
    yn = (1 - y) * 2 + x
    dn = (1 - y) * 2 + 1 - x
    planes = [plane, xn, yn, dn]

    def ex(zz, pp):
        return {"expert": zz * 4 + pp}

    other = {"tensor": 1 - c}

    def rows(zz, pp, n=1):
        return pl.ds(pl.multiple_of((zz * 4 + pp) * T, T), n * T)

    def remote(src, dst, ssem, rsem, dev):
        return pltpu.make_async_remote_copy(
            src_ref=src, dst_ref=dst, send_sem=ssem, recv_sem=rsem,
            device_id=dev, device_id_type=MESH,
        )

    w_g = pltpu.make_async_copy(gate_hbm.at[0], gu.at[0], wsem.at[0])
    w_u = pltpu.make_async_copy(up_hbm.at[0], gu.at[1], wsem.at[1])
    w_d = pltpu.make_async_copy(
        down_hbm.at[0, :, pl.ds(pl.multiple_of(c * DH, DH), DH)], dw.at[c], wsem.at[2]
    )
    w_g.start()
    w_u.start()

    barrier = pltpu.get_barrier_semaphore()
    peers = [ex(zd[1], plane), ex(zd[2], plane), ex(zd[3], plane),
             ex(z, xn), ex(z, yn), ex(z, dn), other]
    for p in peers:
        pl.semaphore_signal(barrier, inc=1, device_id=p, device_id_type=MESH)

    lane = lax.broadcasted_iota(jnp.int32, (T, 128), 1)
    table = jnp.zeros((T, 128), F32)
    for k in range(ids_ref.shape[1]):
        table = table + jnp.where(ids_ref[:, k:k + 1] == lane, rw_ref[:, k:k + 1], 0.0)
    high = table.astype(BF16)
    low = (table - high.astype(F32)).astype(BF16)
    own = rows(z, plane)
    xg[c, own, :DH] = tok_ref[...]
    xg[c, own, DH:] = jnp.where(c == 0, high.astype(F32), low.astype(F32)).astype(BF16)

    pl.semaphore_wait(barrier, len(peers))

    started = []

    def go(copy):
        copy.start()
        started.append(copy)
        return copy

    def block(zz, pp):
        return xg.at[c, rows(zz, pp)]

    def block_other(zz, pp):
        return xg.at[1 - c, rows(zz, pp)]

    for d in (1, 2, 3):
        go(remote(block(z, plane), block(z, plane), zs.at[d], zr.at[d], ex(zd[d], plane)))

    dcopy = remote(
        down_hbm.at[0, :, pl.ds(pl.multiple_of((1 - c) * DH, DH), DH)], dw.at[c], dws, dwr, other
    )

    def fan(d):
        b = block(zd[d], plane)
        go(remote(b, b, xs.at[d], xr.at[d], ex(z, xn)))
        go(remote(b, b, ys.at[d], yr.at[d], ex(z, yn)))
        go(remote(b, b, ps.at[d, 0], pr.at[d, 0], other))

    def second(d):
        bx = block(zd[d], xn)
        by = block(zd[d], yn)
        if d % 2 == 0:
            remote(bx, bx, xs.at[d], xr.at[d], ex(z, xn)).wait_recv()
            go(remote(bx, bx, ds.at[d], dr.at[d], ex(z, yn)))
            go(remote(bx, bx, ps.at[d, 1], pr.at[d, 1], other))
            remote(by, by, ys.at[d], yr.at[d], ex(z, yn)).wait_recv()
            go(remote(by, by, ps.at[d, 2], pr.at[d, 2], other))
        else:
            remote(by, by, ys.at[d], yr.at[d], ex(z, yn)).wait_recv()
            go(remote(by, by, ds.at[d], dr.at[d], ex(z, xn)))
            go(remote(by, by, ps.at[d, 2], pr.at[d, 2], other))
            remote(bx, bx, xs.at[d], xr.at[d], ex(z, xn)).wait_recv()
            go(remote(bx, bx, ps.at[d, 1], pr.at[d, 1], other))

    def third(d):
        b = block(zd[d], dn)
        remote(b, b, ds.at[d], dr.at[d], ex(z, dn)).wait_recv()
        go(remote(b, b, ps.at[d, 3], pr.at[d, 3], other))

    def zwait(d):
        b = block(zd[d], plane)
        remote(b, b, zs.at[d], zr.at[d], ex(zd[d], plane)).wait_recv()

    def others(d):
        for j in range(4):
            b = block_other(zd[d], planes[j])
            remote(b, b, ps.at[d, j], pr.at[d, j], other).wait_recv()

    fan(0)
    go(dcopy)
    w_d.start()
    zwait(1)
    fan(1)
    second(0)
    zwait(2)
    fan(2)
    second(1)
    zwait(3)
    fan(3)
    third(0)
    third(1)
    others(0)
    others(1)
    w_g.wait()
    w_u.wait()

    half = 8 * T

    def up_phase(i, r0):
        rr = pl.ds(pl.multiple_of(r0, half), half)
        g = jnp.dot(xg[0, rr, :DH], gu[0, :DH, :], preferred_element_type=F32)
        g = g + jnp.dot(xg[1, rr, :DH], gu[0, DH:, :], preferred_element_type=F32)
        u = jnp.dot(xg[0, rr, :DH], gu[1, :DH, :], preferred_element_type=F32)
        u = u + jnp.dot(xg[1, rr, :DH], gu[1, DH:, :], preferred_element_type=F32)
        hid[c, rr, :] = (g / (1.0 + jnp.exp(-g)) * u).astype(BF16)
        h = hid.at[c, rr]
        go(remote(h, h, hs.at[i], hr.at[i], other))

    def down_phase(i, r0):
        rr = pl.ds(pl.multiple_of(r0, half), half)
        h = hid.at[1 - c, rr]
        remote(h, h, hs.at[i], hr.at[i], other).wait_recv()
        col = lax.broadcasted_iota(jnp.int32, (half, 128), 1)
        wt = xg[0, rr, DH:].astype(F32) + xg[1, rr, DH:].astype(F32)
        wt = jnp.sum(jnp.where(col == me, wt, 0.0), axis=1, keepdims=True)
        v = jnp.dot(hid[0, rr, :], dw[0], preferred_element_type=F32)
        v = v + jnp.dot(hid[1, rr, :], dw[1], preferred_element_type=F32)
        ysend[rr, :] = (v * wt).astype(BF16)

    def slot(j, d):
        return p1.at[pl.ds(((j - 1) * 4 + d) * T, T)]

    def send_plane(d):
        for j in (1, 2, 3):
            go(remote(ysend.at[rows(zd[d], planes[j])], slot(j, d),
                      as_.at[j - 1, d], ar.at[j - 1, d], ex(z, planes[j])))

    def reduce_plane(d):
        total = ysend[rows(zd[d], plane), :].astype(F32)
        for j in (1, 2, 3):
            s = slot(j, d)
            remote(s, s, as_.at[j - 1, d], ar.at[j - 1, d], ex(z, planes[j])).wait_recv()
            total = total + s[...].astype(F32)
        return total

    ra = (z // 2) * half
    rb = half - ra
    up_phase(0, ra)
    second(2)
    second(3)
    third(2)
    third(3)
    w_d.wait()
    dcopy.wait_recv()
    down_phase(0, ra)
    send_plane(1)
    others(2)
    others(3)
    up_phase(1, rb)
    down_phase(1, rb)
    send_plane(2)
    send_plane(3)
    send_plane(0)
    for d in (1, 2, 3):
        p2s[d - 1] = reduce_plane(d).astype(BF16)
        go(remote(p2s.at[d - 1], p2r.at[d - 1], bs.at[d - 1], br.at[d - 1], ex(zd[d], plane)))
    total = reduce_plane(0)
    for d in (1, 2, 3):
        s = p2r.at[d - 1]
        remote(s, s, bs.at[d - 1], br.at[d - 1], ex(zd[d], plane)).wait_recv()
        total = total + s[...].astype(F32)
    out_ref[...] = total.astype(BF16)
    for copy in started:
        copy.wait_send()


def fused(tokens, expert_ids, route_weights, gate_weight, up_weight, down_weight):
    T, DH = tokens.shape
    F = gate_weight.shape[2]
    D = gate_weight.shape[1]
    R = 16 * T
    vmem = pl.BlockSpec(memory_space=pltpu.VMEM)
    hbm = pl.BlockSpec(memory_space=pltpu.HBM)
    dma = pltpu.SemaphoreType.DMA
    return pl.pallas_call(
        kernel,
        out_shape=jax.ShapeDtypeStruct((T, DH), BF16),
        in_specs=[vmem, vmem, vmem, hbm, hbm, hbm],
        out_specs=vmem,
        scratch_shapes=[
            pltpu.VMEM((2, R, DH + 128), BF16),
            pltpu.VMEM((2, D, F), BF16),
            pltpu.VMEM((2, F, DH), BF16),
            pltpu.VMEM((2, R, F), BF16),
            pltpu.VMEM((R, DH), BF16),
            pltpu.VMEM((12 * T, DH), BF16),
            pltpu.VMEM((3, T, DH), BF16),
            pltpu.VMEM((3, T, DH), BF16),
            dma((3,)),
            dma((4,)), dma((4,)),
            dma((4,)), dma((4,)),
            dma((4,)), dma((4,)),
            dma((4,)), dma((4,)),
            dma((4, 4)), dma((4, 4)),
            dma, dma,
            dma((2,)), dma((2,)),
            dma((3, 4)), dma((3, 4)),
            dma((3,)), dma((3,)),
        ],
        compiler_params=pltpu.CompilerParams(
            collective_id=0, has_side_effects=True, vmem_limit_bytes=40 * 1024 * 1024
        ),
        cost_estimate=pl.CostEstimate(
            flops=2 * R * D * F * 3, bytes_accessed=6 * D * F, transcendentals=R * F
        ),
    )(tokens, expert_ids, route_weights, gate_weight, up_weight, down_weight)


def solution(mesh):
    in_specs = (
        P(("groups", "expert"), "tensor"),
        P(("groups", "expert"), None),
        P(("groups", "expert"), None),
        P("expert", None, "tensor"),
        P("expert", None, "tensor"),
        P("expert", "tensor", None),
    )
    out_specs = P(("groups", "expert"), "tensor")
    small = mesh.shape["groups"] == 1 and mesh.shape["expert"] == 16 and mesh.shape["tensor"] == 2
    return jax.shard_map(
        fused if small else per_device,
        mesh=mesh, in_specs=in_specs, out_specs=out_specs, check_vma=False,
    )
```

```python
import functools

import jax
import jax.numpy as jnp
from jax import lax
from jax.experimental import pallas as pl
from jax.experimental.pallas import tpu as pltpu
from jax.sharding import PartitionSpec as P

MESH = pl.DeviceIdType.MESH
BF16 = jnp.bfloat16
F32 = jnp.float32


def per_device(tokens, expert_ids, route_weights, gate_weight, up_weight, down_weight):
    tok_rows = tokens.shape[0]
    top_count = expert_ids.shape[1]
    expert_count = lax.axis_size("expert")
    capacity = min(
        tok_rows, max(2, (4 * tok_rows * top_count + 3 * expert_count - 1) // (3 * expert_count))
    )
    expert_range = jnp.arange(expert_count, dtype=jnp.int32)
    member_of = (expert_ids[:, :, None] == expert_range[None, None, :]).astype(jnp.int32)
    tallies = jnp.sum(member_of, axis=1)
    preceding = jnp.cumsum(tallies, axis=0) - tallies
    slot_index = jnp.sum(member_of * preceding[:, None, :], axis=-1)
    target_row = expert_ids * capacity + slot_index
    row_index = jnp.arange(expert_count * capacity, dtype=jnp.int32)
    placing = jnp.any(target_row[None, :, :] == row_index[:, None, None], axis=-1).astype(
        jnp.bfloat16
    )
    outgoing = jnp.dot(placing, tokens, preferred_element_type=jnp.float32).astype(jnp.bfloat16)
    outgoing = outgoing.reshape(expert_count, capacity, tokens.shape[1])
    incoming = lax.all_to_all(outgoing, "expert", split_axis=0, concat_axis=0, tiled=True)
    incoming = lax.all_gather(incoming, "tensor", axis=2, tiled=True)
    senders = incoming.shape[0]
    items = incoming.shape[1]
    stacked = incoming.reshape(senders * items, incoming.shape[2])
    gate_act = jnp.dot(stacked, gate_weight[0], preferred_element_type=jnp.float32)
    up_act = jnp.dot(stacked, up_weight[0], preferred_element_type=jnp.float32)
    hidden = (jax.nn.silu(gate_act) * up_act).astype(jnp.bfloat16)
    partial_value = jnp.dot(hidden, down_weight[0], preferred_element_type=jnp.float32)
    partial_value = partial_value.reshape(senders, items, partial_value.shape[1])
    returned = lax.all_to_all(partial_value, "expert", split_axis=0, concat_axis=0, tiled=True)
    returned = returned.reshape(expert_count * capacity, returned.shape[2])
    picked = jnp.take(returned, target_row.reshape(-1), axis=0).reshape(
        tok_rows, top_count, returned.shape[1]
    )
    mixed = jnp.sum(route_weights[:, :, None] * picked, axis=1)
    mixed = lax.psum_scatter(mixed, "tensor", scatter_dimension=1, tiled=True)
    return mixed.astype(jnp.bfloat16)


def kernel(
    tok_hbm, ids_hbm, rw_hbm, gate_hbm, up_hbm, down_hbm, out_ref,
    tok_ref, ids_ref, rw_ref, xg, gu, dw, hid, ysend, p1, p2s, p2r,
    wsem, zs, zr, xs, xr, ys, yr, ds, dr, ps, pr, dws, dwr, hs, hr, as_, ar, bs, br,
):
    T = tok_hbm.shape[0]
    DH = tok_hbm.shape[1]
    me = lax.axis_index("expert")
    c = lax.axis_index("tensor")
    x = me % 2
    y = (me // 2) % 2
    z = me // 4
    zd = [z, z + 1 - 2 * (z % 2), (z + 2) % 4, 3 - z]
    plane = y * 2 + x
    xn = y * 2 + 1 - x
    yn = (1 - y) * 2 + x
    dn = (1 - y) * 2 + 1 - x
    planes = [plane, xn, yn, dn]

    def ex(zz, pp):
        return {"expert": zz * 4 + pp}

    other = {"tensor": 1 - c}

    def rows(zz, pp, n=1):
        return pl.ds(pl.multiple_of((zz * 4 + pp) * T, T), n * T)

    def remote(src, dst, ssem, rsem, dev):
        return pltpu.make_async_remote_copy(
            src_ref=src, dst_ref=dst, send_sem=ssem, recv_sem=rsem,
            device_id=dev, device_id_type=MESH,
        )

    small = [
        pltpu.make_async_copy(a, b, wsem.at[3 + i])
        for i, (a, b) in enumerate(((ids_hbm, ids_ref), (rw_hbm, rw_ref), (tok_hbm, tok_ref)))
    ]
    for copy in small:
        copy.start()
    w_g = pltpu.make_async_copy(gate_hbm.at[0], gu.at[0], wsem.at[0])
    w_u = pltpu.make_async_copy(up_hbm.at[0], gu.at[1], wsem.at[1])
    w_d = pltpu.make_async_copy(
        down_hbm.at[0, :, pl.ds(pl.multiple_of(c * DH, DH), DH)], dw.at[c], wsem.at[2]
    )

    barrier = pltpu.get_barrier_semaphore()
    peers = [ex(zd[1], plane), ex(zd[2], plane), ex(zd[3], plane),
             ex(z, xn), ex(z, yn), ex(z, dn), other]
    for p in peers:
        pl.semaphore_signal(barrier, inc=1, device_id=p, device_id_type=MESH)

    w_g.start()
    w_u.start()
    w_d.start()

    for copy in small:
        copy.wait()
    expert = lax.broadcasted_iota(jnp.int32, (16, T), 0)
    table = jnp.zeros((16, T), F32)
    for k in range(ids_ref.shape[0]):
        table = table + jnp.where(ids_ref[k:k + 1, :] == expert, rw_ref[k:k + 1, :], 0.0)
    table = jnp.pad(table, ((0, 112), (0, 128 - T))).T[:T]
    high = table.astype(BF16)
    low = (table - high.astype(F32)).astype(BF16)
    own = rows(z, plane)
    xg[c, own, :DH] = tok_ref[...]
    xg[c, own, DH:] = jnp.where(c == 0, high.astype(F32), low.astype(F32)).astype(BF16)

    pl.semaphore_wait(barrier, len(peers))

    started = []

    def go(copy):
        copy.start()
        started.append(copy)
        return copy

    def block(zz, pp):
        return xg.at[c, rows(zz, pp)]

    def block_other(zz, pp):
        return xg.at[1 - c, rows(zz, pp)]

    for d in (1, 2, 3):
        go(remote(block(z, plane), block(z, plane), zs.at[d], zr.at[d], ex(zd[d], plane)))

    dcopy = remote(
        down_hbm.at[0, :, pl.ds(pl.multiple_of((1 - c) * DH, DH), DH)], dw.at[c], dws, dwr, other
    )

    def fan(d):
        b = block(zd[d], plane)
        go(remote(b, b, xs.at[d], xr.at[d], ex(z, xn)))
        go(remote(b, b, ys.at[d], yr.at[d], ex(z, yn)))
        go(remote(b, b, ps.at[d, 0], pr.at[d, 0], other))

    def second(d):
        bx = block(zd[d], xn)
        by = block(zd[d], yn)
        if d % 2 == 0:
            remote(bx, bx, xs.at[d], xr.at[d], ex(z, xn)).wait_recv()
            go(remote(bx, bx, ds.at[d], dr.at[d], ex(z, yn)))
            go(remote(bx, bx, ps.at[d, 1], pr.at[d, 1], other))
            remote(by, by, ys.at[d], yr.at[d], ex(z, yn)).wait_recv()
            go(remote(by, by, ps.at[d, 2], pr.at[d, 2], other))
        else:
            remote(by, by, ys.at[d], yr.at[d], ex(z, yn)).wait_recv()
            go(remote(by, by, ds.at[d], dr.at[d], ex(z, xn)))
            go(remote(by, by, ps.at[d, 2], pr.at[d, 2], other))
            remote(bx, bx, xs.at[d], xr.at[d], ex(z, xn)).wait_recv()
            go(remote(bx, bx, ps.at[d, 1], pr.at[d, 1], other))

    def third(d):
        b = block(zd[d], dn)
        remote(b, b, ds.at[d], dr.at[d], ex(z, dn)).wait_recv()
        go(remote(b, b, ps.at[d, 3], pr.at[d, 3], other))

    def zwait(d):
        b = block(zd[d], plane)
        remote(b, b, zs.at[d], zr.at[d], ex(zd[d], plane)).wait_recv()

    def others(d):
        for j in range(4):
            b = block_other(zd[d], planes[j])
            remote(b, b, ps.at[d, j], pr.at[d, j], other).wait_recv()

    fan(0)
    go(dcopy)
    zwait(1)
    fan(1)
    second(0)
    zwait(2)
    fan(2)
    second(1)
    zwait(3)
    fan(3)
    third(0)
    third(1)
    others(0)
    others(1)
    w_g.wait()
    w_u.wait()

    half = 8 * T

    def up_phase(i, r0):
        rr = pl.ds(pl.multiple_of(r0, half), half)
        g = jnp.dot(xg[0, rr, :DH], gu[0, :DH, :], preferred_element_type=F32)
        g = g + jnp.dot(xg[1, rr, :DH], gu[0, DH:, :], preferred_element_type=F32)
        u = jnp.dot(xg[0, rr, :DH], gu[1, :DH, :], preferred_element_type=F32)
        u = u + jnp.dot(xg[1, rr, :DH], gu[1, DH:, :], preferred_element_type=F32)
        hid[c, rr, :] = (g / (1.0 + jnp.exp(-g)) * u).astype(BF16)
        h = hid.at[c, rr]
        go(remote(h, h, hs.at[i], hr.at[i], other))

    def down_phase(i, r0):
        rr = pl.ds(pl.multiple_of(r0, half), half)
        h = hid.at[1 - c, rr]
        remote(h, h, hs.at[i], hr.at[i], other).wait_recv()
        col = lax.broadcasted_iota(jnp.int32, (half, 128), 1)
        wt = xg[0, rr, DH:].astype(F32) + xg[1, rr, DH:].astype(F32)
        wt = jnp.sum(jnp.where(col == me, wt, 0.0), axis=1, keepdims=True)
        v = jnp.dot(hid[0, rr, :], dw[0], preferred_element_type=F32)
        v = v + jnp.dot(hid[1, rr, :], dw[1], preferred_element_type=F32)
        ysend[rr, :] = (v * wt).astype(BF16)

    def slot(j, d):
        return p1.at[pl.ds(((j - 1) * 4 + d) * T, T)]

    def send_plane(d):
        for j in (1, 2, 3):
            go(remote(ysend.at[rows(zd[d], planes[j])], slot(j, d),
                      as_.at[j - 1, d], ar.at[j - 1, d], ex(z, planes[j])))

    def reduce_plane(d):
        total = ysend[rows(zd[d], plane), :].astype(F32)
        for j in (1, 2, 3):
            s = slot(j, d)
            remote(s, s, as_.at[j - 1, d], ar.at[j - 1, d], ex(z, planes[j])).wait_recv()
            total = total + s[...].astype(F32)
        return total

    ra = (z // 2) * half
    rb = half - ra
    up_phase(0, ra)
    second(2)
    second(3)
    third(2)
    third(3)
    w_d.wait()
    dcopy.wait_recv()
    down_phase(0, ra)
    send_plane(1)
    others(2)
    others(3)
    up_phase(1, rb)
    down_phase(1, rb)
    send_plane(2)
    send_plane(3)
    send_plane(0)
    for d in (1, 2, 3):
        p2s[d - 1] = reduce_plane(d).astype(BF16)
        go(remote(p2s.at[d - 1], p2r.at[d - 1], bs.at[d - 1], br.at[d - 1], ex(zd[d], plane)))
    total = reduce_plane(0)
    for d in (1, 2, 3):
        s = p2r.at[d - 1]
        remote(s, s, bs.at[d - 1], br.at[d - 1], ex(zd[d], plane)).wait_recv()
        total = total + s[...].astype(F32)
    out_ref[...] = total.astype(BF16)
    for copy in started:
        copy.wait_send()


def fused(tokens, expert_ids, route_weights, gate_weight, up_weight, down_weight):
    T, DH = tokens.shape
    K = expert_ids.shape[1]
    F = gate_weight.shape[2]
    D = gate_weight.shape[1]
    R = 16 * T
    vmem = pl.BlockSpec(memory_space=pltpu.VMEM)
    hbm = pl.BlockSpec(memory_space=pltpu.HBM)
    dma = pltpu.SemaphoreType.DMA
    return pl.pallas_call(
        kernel,
        out_shape=jax.ShapeDtypeStruct((T, DH), BF16),
        in_specs=[hbm] * 6,
        out_specs=vmem,
        scratch_shapes=[
            pltpu.VMEM((T, DH), BF16),
            pltpu.VMEM((K, T), jnp.int32),
            pltpu.VMEM((K, T), F32),
            pltpu.VMEM((2, R, DH + 128), BF16),
            pltpu.VMEM((2, D, F), BF16),
            pltpu.VMEM((2, F, DH), BF16),
            pltpu.VMEM((2, R, F), BF16),
            pltpu.VMEM((R, DH), BF16),
            pltpu.VMEM((12 * T, DH), BF16),
            pltpu.VMEM((3, T, DH), BF16),
            pltpu.VMEM((3, T, DH), BF16),
            dma((6,)),
            dma((4,)), dma((4,)),
            dma((4,)), dma((4,)),
            dma((4,)), dma((4,)),
            dma((4,)), dma((4,)),
            dma((4, 4)), dma((4, 4)),
            dma, dma,
            dma((2,)), dma((2,)),
            dma((3, 4)), dma((3, 4)),
            dma((3,)), dma((3,)),
        ],
        compiler_params=pltpu.CompilerParams(
            collective_id=0, has_side_effects=True, vmem_limit_bytes=60 * 1024 * 1024
        ),
        cost_estimate=pl.CostEstimate(
            flops=2 * R * D * F * 3, bytes_accessed=6 * D * F, transcendentals=R * F
        ),
    )(tokens, expert_ids.T, route_weights.T, gate_weight, up_weight, down_weight)


def solution(mesh):
    in_specs = (
        P(("groups", "expert"), "tensor"),
        P(("groups", "expert"), None),
        P(("groups", "expert"), None),
        P("expert", None, "tensor"),
        P("expert", None, "tensor"),
        P("expert", "tensor", None),
    )
    out_specs = P(("groups", "expert"), "tensor")
    small = mesh.shape["groups"] == 1 and mesh.shape["expert"] == 16 and mesh.shape["tensor"] == 2
    return jax.shard_map(
        fused if small else per_device,
        mesh=mesh, in_specs=in_specs, out_specs=out_specs, check_vma=False,
    )
```

```python
import functools

import jax
import jax.numpy as jnp
from jax import lax
from jax.experimental import pallas as pl
from jax.experimental.pallas import tpu as pltpu
from jax.sharding import PartitionSpec as P

MESH = pl.DeviceIdType.MESH
BF16 = jnp.bfloat16
F32 = jnp.float32


def per_device(tokens, expert_ids, route_weights, gate_weight, up_weight, down_weight):
    tok_rows = tokens.shape[0]
    top_count = expert_ids.shape[1]
    expert_count = lax.axis_size("expert")
    capacity = min(
        tok_rows, max(2, (4 * tok_rows * top_count + 3 * expert_count - 1) // (3 * expert_count))
    )
    expert_range = jnp.arange(expert_count, dtype=jnp.int32)
    member_of = (expert_ids[:, :, None] == expert_range[None, None, :]).astype(jnp.int32)
    tallies = jnp.sum(member_of, axis=1)
    preceding = jnp.cumsum(tallies, axis=0) - tallies
    slot_index = jnp.sum(member_of * preceding[:, None, :], axis=-1)
    target_row = expert_ids * capacity + slot_index
    row_index = jnp.arange(expert_count * capacity, dtype=jnp.int32)
    placing = jnp.any(target_row[None, :, :] == row_index[:, None, None], axis=-1).astype(
        jnp.bfloat16
    )
    outgoing = jnp.dot(placing, tokens, preferred_element_type=jnp.float32).astype(jnp.bfloat16)
    outgoing = outgoing.reshape(expert_count, capacity, tokens.shape[1])
    incoming = lax.all_to_all(outgoing, "expert", split_axis=0, concat_axis=0, tiled=True)
    incoming = lax.all_gather(incoming, "tensor", axis=2, tiled=True)
    senders = incoming.shape[0]
    items = incoming.shape[1]
    stacked = incoming.reshape(senders * items, incoming.shape[2])
    gate_act = jnp.dot(stacked, gate_weight[0], preferred_element_type=jnp.float32)
    up_act = jnp.dot(stacked, up_weight[0], preferred_element_type=jnp.float32)
    hidden = (jax.nn.silu(gate_act) * up_act).astype(jnp.bfloat16)
    partial_value = jnp.dot(hidden, down_weight[0], preferred_element_type=jnp.float32)
    partial_value = partial_value.reshape(senders, items, partial_value.shape[1])
    returned = lax.all_to_all(partial_value, "expert", split_axis=0, concat_axis=0, tiled=True)
    returned = returned.reshape(expert_count * capacity, returned.shape[2])
    picked = jnp.take(returned, target_row.reshape(-1), axis=0).reshape(
        tok_rows, top_count, returned.shape[1]
    )
    mixed = jnp.sum(route_weights[:, :, None] * picked, axis=1)
    mixed = lax.psum_scatter(mixed, "tensor", scatter_dimension=1, tiled=True)
    return mixed.astype(jnp.bfloat16)


def kernel(
    tok_hbm, ids_hbm, rw_hbm, gate_hbm, up_hbm, down_hbm, out_ref,
    tok_ref, ids_ref, rw_ref, xg, gu, dw, hid, ysend, p1, p2s, p2r,
    wsem, zs, zr, xs, xr, ys, yr, ds, dr, ps, pr, dws, dwr, hs, hr, as_, ar, bs, br,
):
    T = tok_hbm.shape[0]
    DH = tok_hbm.shape[1]
    me = lax.axis_index("expert")
    c = lax.axis_index("tensor")
    x = me % 2
    y = (me // 2) % 2
    z = me // 4
    zd = [z, z + 1 - 2 * (z % 2), 2 - z // 2, 3 - 3 * (z // 2)]
    plane = y * 2 + x
    xn = y * 2 + 1 - x
    yn = (1 - y) * 2 + x
    dn = (1 - y) * 2 + 1 - x
    planes = [plane, xn, yn, dn]

    def ex(zz, pp):
        return {"expert": zz * 4 + pp}

    other = {"tensor": 1 - c}

    def rows(zz, pp, n=1):
        return pl.ds(pl.multiple_of((zz * 4 + pp) * T, T), n * T)

    def remote(src, dst, ssem, rsem, dev):
        return pltpu.make_async_remote_copy(
            src_ref=src, dst_ref=dst, send_sem=ssem, recv_sem=rsem,
            device_id=dev, device_id_type=MESH,
        )

    small = [
        pltpu.make_async_copy(a, b, wsem.at[3 + i])
        for i, (a, b) in enumerate(((ids_hbm, ids_ref), (rw_hbm, rw_ref), (tok_hbm, tok_ref)))
    ]
    for copy in small:
        copy.start()
    w_g = pltpu.make_async_copy(gate_hbm.at[0], gu.at[0], wsem.at[0])
    w_u = pltpu.make_async_copy(up_hbm.at[0], gu.at[1], wsem.at[1])
    w_d = pltpu.make_async_copy(
        down_hbm.at[0, :, pl.ds(pl.multiple_of(c * DH, DH), DH)], dw.at[c], wsem.at[2]
    )

    barrier = pltpu.get_barrier_semaphore()
    peers = [ex(zd[1], plane), ex(zd[2], plane), ex(zd[3], plane),
             ex(z, xn), ex(z, yn), ex(z, dn), other]
    for p in peers:
        pl.semaphore_signal(barrier, inc=1, device_id=p, device_id_type=MESH)

    w_g.start()
    w_u.start()
    w_d.start()

    for copy in small:
        copy.wait()
    expert = lax.broadcasted_iota(jnp.int32, (16, T), 0)
    table = jnp.zeros((16, T), F32)
    for k in range(ids_ref.shape[0]):
        table = table + jnp.where(ids_ref[k:k + 1, :] == expert, rw_ref[k:k + 1, :], 0.0)
    table = jnp.pad(table, ((0, 112), (0, 128 - T))).T[:T]
    high = table.astype(BF16)
    low = (table - high.astype(F32)).astype(BF16)
    own = rows(z, plane)
    xg[c, own, :DH] = tok_ref[...]
    xg[c, own, DH:] = jnp.where(c == 0, high.astype(F32), low.astype(F32)).astype(BF16)

    pl.semaphore_wait(barrier, len(peers))

    started = []

    def go(copy):
        copy.start()
        started.append(copy)
        return copy

    def block(zz, pp):
        return xg.at[c, rows(zz, pp)]

    def block_other(zz, pp):
        return xg.at[1 - c, rows(zz, pp)]

    for d in (1, 2, 3):
        b = block(z, plane)
        go(remote(b, b, zs.at[d], zr.at[z], ex(zd[d], plane)))

    dcopy = remote(
        down_hbm.at[0, :, pl.ds(pl.multiple_of((1 - c) * DH, DH), DH)], dw.at[c], dws, dwr, other
    )

    sems = [None, (xs, xr), (ys, yr), (ds, dr)]

    def spread(src, d, zz):
        b = block(src, plane)
        for j in (3, 1, 2):
            ss, rs = sems[j]
            go(remote(b, b, ss.at[d], rs.at[d], ex(zz, planes[j])))

    def share(d, j):
        b = block(zd[d], planes[j])
        go(remote(b, b, ps.at[d, j], pr.at[d, j], other))

    def arrive(d):
        for j in (1, 2, 3):
            b = block(zd[d], planes[j])
            ss, rs = sems[j]
            remote(b, b, ss.at[d], rs.at[d], ex(z, planes[j])).wait_recv()
            share(d, j)

    def zwait(d):
        b = block(zd[d], plane)
        remote(b, b, zs.at[0], zr.at[zd[d]], ex(zd[d], plane)).wait_recv()

    def others(d):
        for j in range(4):
            b = block_other(zd[d], planes[j])
            remote(b, b, ps.at[d, j], pr.at[d, j], other).wait_recv()

    spread(z, 0, z)
    share(0, 0)
    zwait(1)
    spread(zd[1], 1, z)
    share(1, 0)
    arrive(0)
    zwait(2)
    spread(zd[2], 2, z)
    share(2, 0)
    zwait(3)
    spread(zd[3], 3, z)
    share(3, 0)
    go(dcopy)
    arrive(1)
    others(0)
    others(1)
    w_g.wait()
    w_u.wait()

    half = 8 * T

    def up_phase(i, r0):
        rr = pl.ds(pl.multiple_of(r0, half), half)
        g = jnp.dot(xg[0, rr, :DH], gu[0, :DH, :], preferred_element_type=F32)
        g = g + jnp.dot(xg[1, rr, :DH], gu[0, DH:, :], preferred_element_type=F32)
        u = jnp.dot(xg[0, rr, :DH], gu[1, :DH, :], preferred_element_type=F32)
        u = u + jnp.dot(xg[1, rr, :DH], gu[1, DH:, :], preferred_element_type=F32)
        hid[c, rr, :] = (g / (1.0 + jnp.exp(-g)) * u).astype(BF16)
        h = hid.at[c, rr]
        go(remote(h, h, hs.at[i], hr.at[i], other))

    def down_phase(i, r0):
        rr = pl.ds(pl.multiple_of(r0, half), half)
        h = hid.at[1 - c, rr]
        remote(h, h, hs.at[i], hr.at[i], other).wait_recv()
        col = lax.broadcasted_iota(jnp.int32, (half, 128), 1)
        wt = xg[0, rr, DH:].astype(F32) + xg[1, rr, DH:].astype(F32)
        wt = jnp.sum(jnp.where(col == me, wt, 0.0), axis=1, keepdims=True)
        v = jnp.dot(hid[0, rr, :], dw[0], preferred_element_type=F32)
        v = v + jnp.dot(hid[1, rr, :], dw[1], preferred_element_type=F32)
        ysend[rr, :] = (v * wt).astype(BF16)

    def slot(j, d):
        return p1.at[pl.ds(((j - 1) * 4 + d) * T, T)]

    def send_plane(d):
        for j in (1, 2, 3):
            go(remote(ysend.at[rows(zd[d], planes[j])], slot(j, d),
                      as_.at[j - 1, d], ar.at[j - 1, d], ex(z, planes[j])))

    def reduce_plane(d):
        total = ysend[rows(zd[d], plane), :].astype(F32)
        for j in (1, 2, 3):
            s = slot(j, d)
            remote(s, s, as_.at[j - 1, d], ar.at[j - 1, d], ex(z, planes[j])).wait_recv()
            total = total + s[...].astype(F32)
        return total

    ra = (z // 2) * half
    rb = half - ra
    up_phase(0, ra)
    arrive(2)
    w_d.wait()
    dcopy.wait_recv()
    down_phase(0, ra)
    send_plane(1)
    send_plane(0)
    arrive(3)
    others(2)
    others(3)
    up_phase(1, rb)
    down_phase(1, rb)
    send_plane(3)
    send_plane(2)
    for d in (1, 3, 2):
        p2s[d - 1] = reduce_plane(d).astype(BF16)
        go(remote(p2s.at[d - 1], p2r.at[z], bs.at[d - 1], br.at[z], ex(zd[d], plane)))
    total = reduce_plane(0)
    for d in (1, 2, 3):
        s = p2r.at[zd[d]]
        remote(s, s, bs.at[d - 1], br.at[zd[d]], ex(zd[d], plane)).wait_recv()
        total = total + s[...].astype(F32)
    out_ref[...] = total.astype(BF16)
    for copy in started:
        copy.wait_send()


def fused(tokens, expert_ids, route_weights, gate_weight, up_weight, down_weight):
    T, DH = tokens.shape
    K = expert_ids.shape[1]
    F = gate_weight.shape[2]
    D = gate_weight.shape[1]
    R = 16 * T
    vmem = pl.BlockSpec(memory_space=pltpu.VMEM)
    hbm = pl.BlockSpec(memory_space=pltpu.HBM)
    dma = pltpu.SemaphoreType.DMA
    return pl.pallas_call(
        kernel,
        out_shape=jax.ShapeDtypeStruct((T, DH), BF16),
        in_specs=[hbm] * 6,
        out_specs=vmem,
        scratch_shapes=[
            pltpu.VMEM((T, DH), BF16),
            pltpu.VMEM((K, T), jnp.int32),
            pltpu.VMEM((K, T), F32),
            pltpu.VMEM((2, R, DH + 128), BF16),
            pltpu.VMEM((2, D, F), BF16),
            pltpu.VMEM((2, F, DH), BF16),
            pltpu.VMEM((2, R, F), BF16),
            pltpu.VMEM((R, DH), BF16),
            pltpu.VMEM((12 * T, DH), BF16),
            pltpu.VMEM((3, T, DH), BF16),
            pltpu.VMEM((4, T, DH), BF16),
            dma((6,)),
            dma((4,)), dma((4,)),
            dma((4,)), dma((4,)),
            dma((4,)), dma((4,)),
            dma((4,)), dma((4,)),
            dma((4, 4)), dma((4, 4)),
            dma, dma,
            dma((2,)), dma((2,)),
            dma((3, 4)), dma((3, 4)),
            dma((3,)), dma((4,)),
        ],
        compiler_params=pltpu.CompilerParams(
            collective_id=0, has_side_effects=True, vmem_limit_bytes=60 * 1024 * 1024
        ),
        cost_estimate=pl.CostEstimate(
            flops=2 * R * D * F * 3, bytes_accessed=6 * D * F, transcendentals=R * F
        ),
    )(tokens, expert_ids.T, route_weights.T, gate_weight, up_weight, down_weight)


def solution(mesh):
    in_specs = (
        P(("groups", "expert"), "tensor"),
        P(("groups", "expert"), None),
        P(("groups", "expert"), None),
        P("expert", None, "tensor"),
        P("expert", None, "tensor"),
        P("expert", "tensor", None),
    )
    out_specs = P(("groups", "expert"), "tensor")
    small = mesh.shape["groups"] == 1 and mesh.shape["expert"] == 16 and mesh.shape["tensor"] == 2
    return jax.shard_map(
        fused if small else per_device,
        mesh=mesh, in_specs=in_specs, out_specs=out_specs, check_vma=False,
    )
```

```python
import functools

import jax
import jax.numpy as jnp
from jax import lax
from jax.experimental import pallas as pl
from jax.experimental.pallas import tpu as pltpu
from jax.sharding import PartitionSpec as P

MESH = pl.DeviceIdType.MESH
BF16 = jnp.bfloat16
F32 = jnp.float32


def per_device(tokens, expert_ids, route_weights, gate_weight, up_weight, down_weight):
    tok_rows = tokens.shape[0]
    top_count = expert_ids.shape[1]
    expert_count = lax.axis_size("expert")
    capacity = min(
        tok_rows, max(2, (4 * tok_rows * top_count + 3 * expert_count - 1) // (3 * expert_count))
    )
    expert_range = jnp.arange(expert_count, dtype=jnp.int32)
    member_of = (expert_ids[:, :, None] == expert_range[None, None, :]).astype(jnp.int32)
    tallies = jnp.sum(member_of, axis=1)
    preceding = jnp.cumsum(tallies, axis=0) - tallies
    slot_index = jnp.sum(member_of * preceding[:, None, :], axis=-1)
    target_row = expert_ids * capacity + slot_index
    row_index = jnp.arange(expert_count * capacity, dtype=jnp.int32)
    placing = jnp.any(target_row[None, :, :] == row_index[:, None, None], axis=-1).astype(
        jnp.bfloat16
    )
    outgoing = jnp.dot(placing, tokens, preferred_element_type=jnp.float32).astype(jnp.bfloat16)
    outgoing = outgoing.reshape(expert_count, capacity, tokens.shape[1])
    incoming = lax.all_to_all(outgoing, "expert", split_axis=0, concat_axis=0, tiled=True)
    incoming = lax.all_gather(incoming, "tensor", axis=2, tiled=True)
    senders = incoming.shape[0]
    items = incoming.shape[1]
    stacked = incoming.reshape(senders * items, incoming.shape[2])
    gate_act = jnp.dot(stacked, gate_weight[0], preferred_element_type=jnp.float32)
    up_act = jnp.dot(stacked, up_weight[0], preferred_element_type=jnp.float32)
    hidden = (jax.nn.silu(gate_act) * up_act).astype(jnp.bfloat16)
    partial_value = jnp.dot(hidden, down_weight[0], preferred_element_type=jnp.float32)
    partial_value = partial_value.reshape(senders, items, partial_value.shape[1])
    returned = lax.all_to_all(partial_value, "expert", split_axis=0, concat_axis=0, tiled=True)
    returned = returned.reshape(expert_count * capacity, returned.shape[2])
    picked = jnp.take(returned, target_row.reshape(-1), axis=0).reshape(
        tok_rows, top_count, returned.shape[1]
    )
    mixed = jnp.sum(route_weights[:, :, None] * picked, axis=1)
    mixed = lax.psum_scatter(mixed, "tensor", scatter_dimension=1, tiled=True)
    return mixed.astype(jnp.bfloat16)


def kernel(
    tok_hbm, ids_hbm, rw_hbm, gate_hbm, up_hbm, down_hbm, out_ref,
    tok_ref, ids_ref, rw_ref, acc, xg, gu, dw, hid, ysend, p1, p2s, p2r,
    wsem, zs, zr, xs, xr, ys, yr, ds, dr, ps, pr, dws, dwr, hs, hr, as_, ar, bs, br,
):
    T = tok_hbm.shape[0]
    DH = tok_hbm.shape[1]
    me = lax.axis_index("expert")
    c = lax.axis_index("tensor")
    x = me % 2
    y = (me // 2) % 2
    z = me // 4
    zd = [z, z + 1 - 2 * (z % 2), 2 - z // 2, 3 - 3 * (z // 2)]
    plane = y * 2 + x
    xn = y * 2 + 1 - x
    yn = (1 - y) * 2 + x
    dn = (1 - y) * 2 + 1 - x
    planes = [plane, xn, yn, dn]

    def ex(zz, pp):
        return {"expert": zz * 4 + pp}

    other = {"tensor": 1 - c}

    def rows(zz, pp, n=1):
        return pl.ds(pl.multiple_of((zz * 4 + pp) * T, T), n * T)

    def remote(src, dst, ssem, rsem, dev):
        return pltpu.make_async_remote_copy(
            src_ref=src, dst_ref=dst, send_sem=ssem, recv_sem=rsem,
            device_id=dev, device_id_type=MESH,
        )

    small = [
        pltpu.make_async_copy(a, b, wsem.at[3 + i])
        for i, (a, b) in enumerate(((ids_hbm, ids_ref), (rw_hbm, rw_ref), (tok_hbm, tok_ref)))
    ]
    for copy in small:
        copy.start()
    w_g = pltpu.make_async_copy(gate_hbm.at[0], gu.at[0], wsem.at[0])
    w_u = pltpu.make_async_copy(up_hbm.at[0], gu.at[1], wsem.at[1])
    w_d = pltpu.make_async_copy(
        down_hbm.at[0, :, pl.ds(pl.multiple_of(c * DH, DH), DH)], dw.at[c], wsem.at[2]
    )

    barrier = pltpu.get_barrier_semaphore()
    peers = [ex(zd[1], plane), ex(zd[2], plane), ex(zd[3], plane),
             ex(z, xn), ex(z, yn), ex(z, dn), other]
    for p in peers:
        pl.semaphore_signal(barrier, inc=1, device_id=p, device_id_type=MESH)

    w_g.start()
    w_u.start()
    w_d.start()

    for copy in small:
        copy.wait()
    expert = lax.broadcasted_iota(jnp.int32, (16, T), 0)
    table = jnp.zeros((16, T), F32)
    for k in range(ids_ref.shape[0]):
        table = table + jnp.where(ids_ref[k:k + 1, :] == expert, rw_ref[k:k + 1, :], 0.0)
    table = jnp.pad(table, ((0, 112), (0, 128 - T))).T[:T]
    high = table.astype(BF16)
    low = (table - high.astype(F32)).astype(BF16)
    own = rows(z, plane)
    xg[c, own, :DH] = tok_ref[...]
    xg[c, own, DH:] = jnp.where(c == 0, high.astype(F32), low.astype(F32)).astype(BF16)

    pl.semaphore_wait(barrier, len(peers))

    started = []

    def go(copy):
        copy.start()
        started.append(copy)
        return copy

    def block(zz, pp):
        return xg.at[c, rows(zz, pp)]

    def block_other(zz, pp):
        return xg.at[1 - c, rows(zz, pp)]

    for d in (1, 2, 3):
        b = block(z, plane)
        go(remote(b, b, zs.at[d], zr.at[z], ex(zd[d], plane)))

    dcopy = remote(
        down_hbm.at[0, :, pl.ds(pl.multiple_of((1 - c) * DH, DH), DH)], dw.at[c], dws, dwr, other
    )

    sems = [None, (xs, xr), (ys, yr), (ds, dr)]

    def spread(src, d, zz):
        b = block(src, plane)
        for j in (3, 1, 2):
            ss, rs = sems[j]
            go(remote(b, b, ss.at[d], rs.at[d], ex(zz, planes[j])))

    def share(d, j):
        b = block(zd[d], planes[j])
        go(remote(b, b, ps.at[d, j], pr.at[d, j], other))

    def arrive(d):
        for j in (1, 2, 3):
            b = block(zd[d], planes[j])
            ss, rs = sems[j]
            remote(b, b, ss.at[d], rs.at[d], ex(z, planes[j])).wait_recv()
            share(d, j)

    def zwait(d):
        b = block(zd[d], plane)
        remote(b, b, zs.at[0], zr.at[zd[d]], ex(zd[d], plane)).wait_recv()

    def others(d):
        for j in range(4):
            b = block_other(zd[d], planes[j])
            remote(b, b, ps.at[d, j], pr.at[d, j], other).wait_recv()

    spread(z, 0, z)
    share(0, 0)
    zwait(1)
    spread(zd[1], 1, z)
    share(1, 0)
    arrive(0)
    zwait(2)
    spread(zd[2], 2, z)
    share(2, 0)
    zwait(3)
    spread(zd[3], 3, z)
    share(3, 0)
    go(dcopy)
    arrive(1)
    w_g.wait()
    w_u.wait()

    half = 8 * T

    own_d = pl.ds(pl.multiple_of(c * DH, DH), DH)
    oth_d = pl.ds(pl.multiple_of((1 - c) * DH, DH), DH)

    def up_phase(i, r0, groups):
        rr = pl.ds(pl.multiple_of(r0, half), half)
        g = jnp.dot(xg[c, rr, :DH], gu[0, own_d, :], preferred_element_type=F32)
        u = jnp.dot(xg[c, rr, :DH], gu[1, own_d, :], preferred_element_type=F32)
        for d in groups:
            others(d)
        g = g + jnp.dot(xg[1 - c, rr, :DH], gu[0, oth_d, :], preferred_element_type=F32)
        u = u + jnp.dot(xg[1 - c, rr, :DH], gu[1, oth_d, :], preferred_element_type=F32)
        hid[c, rr, :] = (g / (1.0 + jnp.exp(-g)) * u).astype(BF16)
        h = hid.at[c, rr]
        go(remote(h, h, hs.at[i], hr.at[i], other))

    def down_phase(i, r0, groups):
        rr = pl.ds(pl.multiple_of(r0, half), half)
        col = lax.broadcasted_iota(jnp.int32, (half, 128), 1)
        wt = xg[0, rr, DH:].astype(F32) + xg[1, rr, DH:].astype(F32)
        wt = jnp.sum(jnp.where(col == me, wt, 0.0), axis=1, keepdims=True)
        acc[rr, :] = jnp.dot(hid[c, rr, :], dw[c], preferred_element_type=F32)
        h = hid.at[1 - c, rr]
        remote(h, h, hs.at[i], hr.at[i], other).wait_recv()
        v = acc[rr, :] + jnp.dot(hid[1 - c, rr, :], dw[1 - c], preferred_element_type=F32)
        ysend[rr, :] = (v * wt).astype(BF16)
        for d in groups:
            send_plane(d)

    def slot(j, d):
        return p1.at[pl.ds(((j - 1) * 4 + d) * T, T)]

    def send_plane(d):
        for j in (3, 1, 2):
            go(remote(ysend.at[rows(zd[d], planes[j])], slot(j, d),
                      as_.at[j - 1, d], ar.at[j - 1, d], ex(z, planes[j])))

    def reduce_plane(d):
        total = ysend[rows(zd[d], plane), :].astype(F32)
        for j in (1, 2, 3):
            s = slot(j, d)
            remote(s, s, as_.at[j - 1, d], ar.at[j - 1, d], ex(z, planes[j])).wait_recv()
            total = total + s[...].astype(F32)
        return total

    ra = (z // 2) * half
    rb = half - ra
    up_phase(0, ra, (0, 1))
    arrive(2)
    w_d.wait()
    dcopy.wait_recv()
    down_phase(0, ra, (1, 0))
    arrive(3)
    up_phase(1, rb, (2, 3))
    down_phase(1, rb, (3, 2))
    for d in (1, 3, 2):
        p2s[d - 1] = reduce_plane(d).astype(BF16)
        go(remote(p2s.at[d - 1], p2r.at[z], bs.at[d - 1], br.at[z], ex(zd[d], plane)))
    total = reduce_plane(0)
    for copy in started[:-3]:
        copy.wait_send()
    for d in (1, 3, 2):
        s = p2r.at[zd[d]]
        remote(s, s, bs.at[d - 1], br.at[zd[d]], ex(zd[d], plane)).wait_recv()
        total = total + s[...].astype(F32)
    out_ref[...] = total.astype(BF16)
    for copy in started[-3:]:
        copy.wait_send()


def fused(tokens, expert_ids, route_weights, gate_weight, up_weight, down_weight):
    T, DH = tokens.shape
    K = expert_ids.shape[1]
    F = gate_weight.shape[2]
    D = gate_weight.shape[1]
    R = 16 * T
    vmem = pl.BlockSpec(memory_space=pltpu.VMEM)
    hbm = pl.BlockSpec(memory_space=pltpu.HBM)
    dma = pltpu.SemaphoreType.DMA
    return pl.pallas_call(
        kernel,
        out_shape=jax.ShapeDtypeStruct((T, DH), BF16),
        in_specs=[hbm] * 6,
        out_specs=vmem,
        scratch_shapes=[
            pltpu.VMEM((T, DH), BF16),
            pltpu.VMEM((K, T), jnp.int32),
            pltpu.VMEM((K, T), F32),
            pltpu.VMEM((R, DH), F32),
            pltpu.VMEM((2, R, DH + 128), BF16),
            pltpu.VMEM((2, D, F), BF16),
            pltpu.VMEM((2, F, DH), BF16),
            pltpu.VMEM((2, R, F), BF16),
            pltpu.VMEM((R, DH), BF16),
            pltpu.VMEM((12 * T, DH), BF16),
            pltpu.VMEM((3, T, DH), BF16),
            pltpu.VMEM((4, T, DH), BF16),
            dma((6,)),
            dma((4,)), dma((4,)),
            dma((4,)), dma((4,)),
            dma((4,)), dma((4,)),
            dma((4,)), dma((4,)),
            dma((4, 4)), dma((4, 4)),
            dma, dma,
            dma((2,)), dma((2,)),
            dma((3, 4)), dma((3, 4)),
            dma((3,)), dma((4,)),
        ],
        compiler_params=pltpu.CompilerParams(
            collective_id=0, has_side_effects=True, vmem_limit_bytes=60 * 1024 * 1024
        ),
        cost_estimate=pl.CostEstimate(
            flops=2 * R * D * F * 3, bytes_accessed=6 * D * F, transcendentals=R * F
        ),
    )(tokens, expert_ids.T, route_weights.T, gate_weight, up_weight, down_weight)


def solution(mesh):
    in_specs = (
        P(("groups", "expert"), "tensor"),
        P(("groups", "expert"), None),
        P(("groups", "expert"), None),
        P("expert", None, "tensor"),
        P("expert", None, "tensor"),
        P("expert", "tensor", None),
    )
    out_specs = P(("groups", "expert"), "tensor")
    small = mesh.shape["groups"] == 1 and mesh.shape["expert"] == 16 and mesh.shape["tensor"] == 2
    return jax.shard_map(
        fused if small else per_device,
        mesh=mesh, in_specs=in_specs, out_specs=out_specs, check_vma=False,
    )
```

```python
import functools

import jax
import jax.numpy as jnp
from jax import lax
from jax.experimental import pallas as pl
from jax.experimental.pallas import tpu as pltpu
from jax.sharding import PartitionSpec as P

MESH = pl.DeviceIdType.MESH
BF16 = jnp.bfloat16
F32 = jnp.float32


def per_device(tokens, expert_ids, route_weights, gate_weight, up_weight, down_weight):
    tok_rows = tokens.shape[0]
    top_count = expert_ids.shape[1]
    expert_count = lax.axis_size("expert")
    capacity = min(
        tok_rows, max(2, (4 * tok_rows * top_count + 3 * expert_count - 1) // (3 * expert_count))
    )
    expert_range = jnp.arange(expert_count, dtype=jnp.int32)
    member_of = (expert_ids[:, :, None] == expert_range[None, None, :]).astype(jnp.int32)
    tallies = jnp.sum(member_of, axis=1)
    preceding = jnp.cumsum(tallies, axis=0) - tallies
    slot_index = jnp.sum(member_of * preceding[:, None, :], axis=-1)
    target_row = expert_ids * capacity + slot_index
    row_index = jnp.arange(expert_count * capacity, dtype=jnp.int32)
    placing = jnp.any(target_row[None, :, :] == row_index[:, None, None], axis=-1).astype(
        jnp.bfloat16
    )
    outgoing = jnp.dot(placing, tokens, preferred_element_type=jnp.float32).astype(jnp.bfloat16)
    outgoing = outgoing.reshape(expert_count, capacity, tokens.shape[1])
    incoming = lax.all_to_all(outgoing, "expert", split_axis=0, concat_axis=0, tiled=True)
    incoming = lax.all_gather(incoming, "tensor", axis=2, tiled=True)
    senders = incoming.shape[0]
    items = incoming.shape[1]
    stacked = incoming.reshape(senders * items, incoming.shape[2])
    gate_act = jnp.dot(stacked, gate_weight[0], preferred_element_type=jnp.float32)
    up_act = jnp.dot(stacked, up_weight[0], preferred_element_type=jnp.float32)
    hidden = (jax.nn.silu(gate_act) * up_act).astype(jnp.bfloat16)
    partial_value = jnp.dot(hidden, down_weight[0], preferred_element_type=jnp.float32)
    partial_value = partial_value.reshape(senders, items, partial_value.shape[1])
    returned = lax.all_to_all(partial_value, "expert", split_axis=0, concat_axis=0, tiled=True)
    returned = returned.reshape(expert_count * capacity, returned.shape[2])
    picked = jnp.take(returned, target_row.reshape(-1), axis=0).reshape(
        tok_rows, top_count, returned.shape[1]
    )
    mixed = jnp.sum(route_weights[:, :, None] * picked, axis=1)
    mixed = lax.psum_scatter(mixed, "tensor", scatter_dimension=1, tiled=True)
    return mixed.astype(jnp.bfloat16)


def kernel(
    tok_hbm, ids_hbm, rw_hbm, gate_hbm, up_hbm, down_hbm, out_ref,
    tok_ref, ids_ref, rw_ref, acc, xg, gu, dw, hid, ysend, p1, p2s, p2r,
    wsem, zs, zr, xs, xr, ys, yr, ds, dr, ps, pr, dws, dwr, hs, hr, as_, ar, bs, br,
):
    T = tok_hbm.shape[0]
    DH = tok_hbm.shape[1]
    me = lax.axis_index("expert")
    c = lax.axis_index("tensor")
    x = me % 2
    y = (me // 2) % 2
    z = me // 4
    zd = [z, z + 1 - 2 * (z % 2), 2 - z // 2, 3 - 3 * (z // 2)]
    plane = y * 2 + x
    xn = y * 2 + 1 - x
    yn = (1 - y) * 2 + x
    dn = (1 - y) * 2 + 1 - x
    planes = [plane, xn, yn, dn]

    def ex(zz, pp):
        return {"expert": zz * 4 + pp}

    other = {"tensor": 1 - c}

    def rows(zz, pp, n=1):
        return pl.ds(pl.multiple_of((zz * 4 + pp) * T, T), n * T)

    def remote(src, dst, ssem, rsem, dev):
        return pltpu.make_async_remote_copy(
            src_ref=src, dst_ref=dst, send_sem=ssem, recv_sem=rsem,
            device_id=dev, device_id_type=MESH,
        )

    small = [
        pltpu.make_async_copy(a, b, wsem.at[3 + i])
        for i, (a, b) in enumerate(((ids_hbm, ids_ref), (rw_hbm, rw_ref), (tok_hbm, tok_ref)))
    ]
    for copy in small:
        copy.start()
    w_g = pltpu.make_async_copy(gate_hbm.at[0], gu.at[0], wsem.at[0])
    w_u = pltpu.make_async_copy(up_hbm.at[0], gu.at[1], wsem.at[1])
    w_d = pltpu.make_async_copy(
        down_hbm.at[0, :, pl.ds(pl.multiple_of(c * DH, DH), DH)], dw.at[c], wsem.at[2]
    )

    barrier = pltpu.get_barrier_semaphore()
    peers = [ex(zd[1], plane), ex(zd[2], plane), ex(zd[3], plane),
             ex(z, xn), ex(z, yn), ex(z, dn), other]
    for p in peers:
        pl.semaphore_signal(barrier, inc=1, device_id=p, device_id_type=MESH)

    w_g.start()
    w_u.start()
    w_d.start()

    for copy in small:
        copy.wait()
    expert = lax.broadcasted_iota(jnp.int32, (16, T), 0)
    table = jnp.zeros((16, T), F32)
    for k in range(ids_ref.shape[0]):
        table = table + jnp.where(ids_ref[k:k + 1, :] == expert, rw_ref[k:k + 1, :], 0.0)
    table = jnp.pad(table, ((0, 112), (0, 128 - T))).T[:T]
    high = table.astype(BF16)
    low = (table - high.astype(F32)).astype(BF16)
    own = rows(z, plane)
    xg[c, own, :DH] = tok_ref[...]
    xg[c, own, DH:] = jnp.where(c == 0, high.astype(F32), low.astype(F32)).astype(BF16)

    pl.semaphore_wait(barrier, len(peers))

    started = []

    def go(copy):
        copy.start()
        started.append(copy)
        return copy

    def block(zz, pp):
        return xg.at[c, rows(zz, pp)]

    def block_other(zz, pp):
        return xg.at[1 - c, rows(zz, pp)]

    for d in (1, 2, 3):
        b = block(z, plane)
        go(remote(b, b, zs.at[d], zr.at[z], ex(zd[d], plane)))

    dcopy = remote(
        down_hbm.at[0, :, pl.ds(pl.multiple_of((1 - c) * DH, DH), DH)], dw.at[c], dws, dwr, other
    )

    sems = [None, (xs, xr), (ys, yr), (ds, dr)]

    def spread(src, d, zz):
        b = block(src, plane)
        for j in (3, 1, 2):
            ss, rs = sems[j]
            go(remote(b, b, ss.at[d], rs.at[d], ex(zz, planes[j])))

    def share(d, j):
        b = block(zd[d], planes[j])
        go(remote(b, b, ps.at[d, j], pr.at[d, j], other))

    def arrive(d):
        for j in (1, 2, 3):
            b = block(zd[d], planes[j])
            ss, rs = sems[j]
            remote(b, b, ss.at[d], rs.at[d], ex(z, planes[j])).wait_recv()
            if d >= 2:
                share(d, j)
        if d < 2:
            b = xg.at[c, rows(zd[d], 0, 4)]
            go(remote(b, b, ps.at[d, 0], pr.at[d, 0], other))

    def zwait(d):
        b = block(zd[d], plane)
        remote(b, b, zs.at[0], zr.at[zd[d]], ex(zd[d], plane)).wait_recv()

    def others(d):
        if d < 2:
            b = xg.at[1 - c, rows(zd[d], 0, 4)]
            remote(b, b, ps.at[d, 0], pr.at[d, 0], other).wait_recv()
            return
        for j in range(4):
            b = block_other(zd[d], planes[j])
            remote(b, b, ps.at[d, j], pr.at[d, j], other).wait_recv()

    spread(z, 0, z)
    zwait(1)
    spread(zd[1], 1, z)
    arrive(0)
    zwait(2)
    spread(zd[2], 2, z)
    share(2, 0)
    zwait(3)
    spread(zd[3], 3, z)
    share(3, 0)
    go(dcopy)
    arrive(1)
    w_g.wait()
    w_u.wait()

    half = 8 * T

    own_d = pl.ds(pl.multiple_of(c * DH, DH), DH)
    oth_d = pl.ds(pl.multiple_of((1 - c) * DH, DH), DH)

    def up_phase(i, r0, groups):
        rr = pl.ds(pl.multiple_of(r0, half), half)
        g = jnp.dot(xg[c, rr, :DH], gu[0, own_d, :], preferred_element_type=F32)
        u = jnp.dot(xg[c, rr, :DH], gu[1, own_d, :], preferred_element_type=F32)
        for d in groups:
            others(d)
        g = g + jnp.dot(xg[1 - c, rr, :DH], gu[0, oth_d, :], preferred_element_type=F32)
        u = u + jnp.dot(xg[1 - c, rr, :DH], gu[1, oth_d, :], preferred_element_type=F32)
        hid[c, rr, :] = (g / (1.0 + jnp.exp(-g)) * u).astype(BF16)
        h = hid.at[c, rr]
        go(remote(h, h, hs.at[i], hr.at[i], other))

    def down_phase(i, r0, groups):
        rr = pl.ds(pl.multiple_of(r0, half), half)
        col = lax.broadcasted_iota(jnp.int32, (half, 128), 1)
        wt = xg[0, rr, DH:].astype(F32) + xg[1, rr, DH:].astype(F32)
        wt = jnp.sum(jnp.where(col == me, wt, 0.0), axis=1, keepdims=True)
        acc[rr, :] = jnp.dot(hid[c, rr, :], dw[c], preferred_element_type=F32)
        h = hid.at[1 - c, rr]
        remote(h, h, hs.at[i], hr.at[i], other).wait_recv()
        v = acc[rr, :] + jnp.dot(hid[1 - c, rr, :], dw[1 - c], preferred_element_type=F32)
        ysend[rr, :] = (v * wt).astype(BF16)
        for d in groups:
            send_plane(d)

    def slot(j, d):
        return p1.at[pl.ds(((j - 1) * 4 + d) * T, T)]

    def send_plane(d):
        for j in (3, 1, 2):
            go(remote(ysend.at[rows(zd[d], planes[j])], slot(j, d),
                      as_.at[j - 1, d], ar.at[j - 1, d], ex(z, planes[j])))

    def reduce_plane(d):
        total = ysend[rows(zd[d], plane), :].astype(F32)
        for j in (1, 2, 3):
            s = slot(j, d)
            remote(s, s, as_.at[j - 1, d], ar.at[j - 1, d], ex(z, planes[j])).wait_recv()
            total = total + s[...].astype(F32)
        return total

    ra = (z // 2) * half
    rb = half - ra
    up_phase(0, ra, (0, 1))
    arrive(2)
    w_d.wait()
    dcopy.wait_recv()
    down_phase(0, ra, (1, 0))
    arrive(3)
    up_phase(1, rb, (2, 3))
    down_phase(1, rb, (3, 2))
    for d in (1, 3, 2):
        p2s[d - 1] = reduce_plane(d).astype(BF16)
        go(remote(p2s.at[d - 1], p2r.at[z], bs.at[d - 1], br.at[z], ex(zd[d], plane)))
    total = reduce_plane(0)
    for copy in started[:-3]:
        copy.wait_send()
    for d in (1, 3, 2):
        s = p2r.at[zd[d]]
        remote(s, s, bs.at[d - 1], br.at[zd[d]], ex(zd[d], plane)).wait_recv()
        total = total + s[...].astype(F32)
    out_ref[...] = total.astype(BF16)
    for copy in started[-3:]:
        copy.wait_send()


def fused(tokens, expert_ids, route_weights, gate_weight, up_weight, down_weight):
    T, DH = tokens.shape
    K = expert_ids.shape[1]
    F = gate_weight.shape[2]
    D = gate_weight.shape[1]
    R = 16 * T
    vmem = pl.BlockSpec(memory_space=pltpu.VMEM)
    hbm = pl.BlockSpec(memory_space=pltpu.HBM)
    dma = pltpu.SemaphoreType.DMA
    return pl.pallas_call(
        kernel,
        out_shape=jax.ShapeDtypeStruct((T, DH), BF16),
        in_specs=[hbm] * 6,
        out_specs=vmem,
        scratch_shapes=[
            pltpu.VMEM((T, DH), BF16),
            pltpu.VMEM((K, T), jnp.int32),
            pltpu.VMEM((K, T), F32),
            pltpu.VMEM((R, DH), F32),
            pltpu.VMEM((2, R, DH + 128), BF16),
            pltpu.VMEM((2, D, F), BF16),
            pltpu.VMEM((2, F, DH), BF16),
            pltpu.VMEM((2, R, F), BF16),
            pltpu.VMEM((R, DH), BF16),
            pltpu.VMEM((12 * T, DH), BF16),
            pltpu.VMEM((3, T, DH), BF16),
            pltpu.VMEM((4, T, DH), BF16),
            dma((6,)),
            dma((4,)), dma((4,)),
            dma((4,)), dma((4,)),
            dma((4,)), dma((4,)),
            dma((4,)), dma((4,)),
            dma((4, 4)), dma((4, 4)),
            dma, dma,
            dma((2,)), dma((2,)),
            dma((3, 4)), dma((3, 4)),
            dma((3,)), dma((4,)),
        ],
        compiler_params=pltpu.CompilerParams(
            collective_id=0, has_side_effects=True, vmem_limit_bytes=60 * 1024 * 1024
        ),
        cost_estimate=pl.CostEstimate(
            flops=2 * R * D * F * 3, bytes_accessed=6 * D * F, transcendentals=R * F
        ),
    )(tokens, expert_ids.T, route_weights.T, gate_weight, up_weight, down_weight)


def solution(mesh):
    in_specs = (
        P(("groups", "expert"), "tensor"),
        P(("groups", "expert"), None),
        P(("groups", "expert"), None),
        P("expert", None, "tensor"),
        P("expert", None, "tensor"),
        P("expert", "tensor", None),
    )
    out_specs = P(("groups", "expert"), "tensor")
    small = mesh.shape["groups"] == 1 and mesh.shape["expert"] == 16 and mesh.shape["tensor"] == 2
    return jax.shard_map(
        fused if small else per_device,
        mesh=mesh, in_specs=in_specs, out_specs=out_specs, check_vma=False,
    )
```
